32 devices in a mesh: loc: 8 (over y, x, core), tm: 4 (over z).
Axes of the slice: x: 2, y: 2, z: 4, core: 2. Of those that a mesh axis runs over, the one named last changes fastest.
Arguments:
- observed: float32 [1024, 512], P('loc', 'tm'), may hold values from -6 to 6
- observed_mask: int32 [1024, 512], P('loc', 'tm'), may hold values 0 or 1
- training_site_positions: float32 [2, 1024], replicated, may hold values from 0 to 1
- time_stamps: float32 [512], replicated, may hold values from 0 to 1
- noise_var: float32 [512], P('tm'), may hold values from 0.2 to 2
- test_coords: float32 [2, 1024], replicated, may hold values from 0 to 1
- site_order: int32 [1024], replicated, may hold values from 0 to 1023, each once
Outputs:
- solver_estimate: float32 [1024, 512], P('loc', 'tm')
- posterior_mean_field: float32 [1024, 512], P('loc', 'tm')
The draws below stay inside these ranges and needn't reach their ends.
Inputs may be any that keep to these rules, and one draw needn't show every extreme that they name: `site_order`: each test site appears once.
All inputs are finite; a program needn't handle non-finite values. No bound on the sum of `observed_mask` on one device may be relied on, other than what follows from the above.
Results may differ from the reference program's by a relative error of at most 0.00022.
Values sent between devices are 32-bit elements; how exact they have to be, the bound alone decides.
A program may use at most 64 MiB of HBM per device.

```python
import math
import jax
import jax.numpy as jnp
from jax import lax

ITERS = 2
LOCS = 1024
TIMES = 512
NTEST = 1024


def place_ends(result, stream_key, smallest, high):
    place = [jax.random.randint(jax.random.fold_in(stream_key, axis), (), 0, length) for axis, length in enumerate(result.shape)]
    longest = result.shape.index(max(result.shape))
    next_to = place[:longest] + [(place[longest] + 1) % result.shape[longest]] + place[longest + 1:]
    return result.at[tuple(place)].set(smallest).at[tuple(next_to)].set(high)


def steps_of(stream_key, shape, pieces, least, high):
    gain, own = 1.0, jax.random.fold_in(stream_key, 6)
    for dim, shards_of in pieces:
        draws = jnp.exp(jax.random.uniform(jax.random.fold_in(own, dim), (shards_of,), jnp.float32, least / len(pieces), high / len(pieces)))
        gain = gain * jnp.repeat(draws, shape[dim] // shards_of).reshape([-1 if axis == dim else 1 for axis in range(len(shape))])
    return gain


def scatter_about(own_key, dims, width, reach, pieces=(), kind=jnp.bfloat16):
    array = jax.random.normal(own_key, dims, jnp.float32) * width
    if len(pieces) > 0:
        array = steps_of(own_key, dims, pieces, -0.22, 0.18) * array
    return jnp.clip(array, min=-reach, max=reach).astype(kind)


def setup_inputs(seed: int = 0) -> dict:
    key_of = jax.random.split(jax.random.key(seed), 8)
    return {
        "observed": scatter_about(key_of[0], (LOCS, TIMES), 1.0, 6.0, ((0, 8), (1, 4)), jnp.float32),
        "observed_mask": place_ends((jax.random.randint(key_of[1], (LOCS, TIMES), 0, 4) < 3).astype(jnp.int32), jax.random.fold_in(key_of[1], 1), 0, 1),
        "training_site_positions": jnp.clip(jax.random.uniform(key_of[2], (2, LOCS), jnp.float32, 0.0, 1.0), 0.0, 1.0),
        "time_stamps": jnp.clip(jax.random.uniform(key_of[3], (TIMES,), jnp.float32, 0.0, 1.0), 0.0, 1.0),
        "noise_var": jnp.clip(jnp.exp(math.log(2.0) - 2.3025851 * jax.random.uniform(key_of[4], (TIMES,), jnp.float32) ** steps_of(key_of[4], (TIMES,), ((0, 4),), -0.2, 0.2)), 0.2, 2.0),
        "test_coords": jnp.clip(jax.random.uniform(key_of[5], (2, NTEST), jnp.float32, 0.0, 1.0), 0.0, 1.0),
        "site_order": jax.random.permutation(key_of[6], NTEST).astype(jnp.int32),
    }


root_three = math.sqrt(3.0)
space_reach = 2.5
time_reach = 5.0
covariance_times_iterate = 0.1

def matern(left_points, right_points, length):
    squared = lax.optimization_barrier(jnp.sum(jnp.square(left_points[:, :, None] - right_points[:, None, :]), axis=0))
    scaled = jnp.sqrt(squared) * (root_three / length)
    return (1.0 + scaled) * jnp.exp(-scaled)

def between_covariance_block(row_points, col_points, right_side, length):
    row_count = row_points.shape[1]
    block_size = math.gcd(row_count, 2048)
    number = row_count // block_size
    blocks = row_points.reshape(row_points.shape[0], number, block_size).transpose(1, 0, 2)

    def one_block(points):
        return jnp.dot(matern(points, col_points, length), right_side, precision=lax.Precision.HIGHEST, preferred_element_type=jnp.float32)
    return lax.map(one_block, blocks).reshape(row_count, right_side.shape[1])

def reference(observed, observed_mask, training_site_positions, time_stamps, noise_var, test_coords, site_order):
    mask_float = observed_mask.astype(jnp.float32)
    planar_correlation_range = space_reach / math.sqrt(LOCS)
    time_length = time_reach / TIMES
    stamp_rows = time_stamps[None, :]
    time_kernel = matern(stamp_rows, stamp_rows, time_length)
    signal_amplitude = covariance_times_iterate

    def operate(direction):
        masked = mask_float * direction
        inner = jnp.dot(masked, time_kernel, precision=lax.Precision.HIGHEST, preferred_element_type=jnp.float32)
        outer = between_covariance_block(training_site_positions, training_site_positions, inner, planar_correlation_range)
        return mask_float * outer * signal_amplitude + direction * noise_var[None, :]
    solver_estimate = jnp.zeros_like(observed)
    residual = mask_float * observed
    direction = residual
    norm_now = jnp.sum(residual * residual)
    for iteration in range(ITERS):
        image = operate(direction)
        step_size = norm_now / jnp.sum(direction * image)
        solver_estimate = solver_estimate + step_size * direction
        residual = residual - step_size * image
        if iteration + 1 < ITERS:
            norm_next = jnp.sum(residual * residual)
            direction = residual + norm_next / norm_now * direction
            norm_now = norm_next
    temporal_observation_grid = jnp.dot(solver_estimate, time_kernel, precision=lax.Precision.HIGHEST, preferred_element_type=jnp.float32)
    unseen_site_positions = test_coords[:, site_order]
    posterior_mean_field = between_covariance_block(unseen_site_positions, training_site_positions, temporal_observation_grid, planar_correlation_range) * signal_amplitude
    return (solver_estimate, posterior_mean_field)
```

```python
import functools
import math

import jax
import jax.numpy as jnp
from jax import lax
from jax.experimental import pallas as pl
from jax.experimental.pallas import tpu as pltpu
from jax.sharding import PartitionSpec as P

MESH = pl.DeviceIdType.MESH
F32 = jnp.float32
BF16 = jnp.bfloat16

root_three = math.sqrt(3.0)
space_reach = 2.5
time_reach = 5.0
amplitude = 0.1
SCALARS = 8


def split(x):
    high = x.astype(BF16)
    return high, (x - high.astype(F32)).astype(BF16)


def dot(a, b):
    return jnp.dot(a, b, preferred_element_type=F32)


def dot3(a_high, a_low, b_high, b_low):
    return dot(a_high, b_high) + (dot(a_high, b_low) + dot(a_low, b_high))


def column_of(row, width):
    return jnp.transpose(jnp.broadcast_to(row, (width, row.shape[1])))


def matern_of(distance, length):
    scaled = distance * (root_three / length)
    return (1.0 + scaled) * jnp.exp(-scaled)


def lane_sums(*arrays):
    sums = [jnp.sum(a, axis=0, keepdims=True) for a in arrays]
    sums.append(jnp.zeros((SCALARS - len(sums), sums[0].shape[1]), F32))
    return jnp.concatenate(sums, axis=0)


def kernel(
    n_loc, n_tm,
    obs, mask, pos, stamps, noise, test, order,
    est, post,
    held, inner, red_t, red_l, ks, kx, kt,
    held_send, held_recv, inner_send, inner_recv, pass_send,
    rt_send, rt_recv, rl_send, rl_recv,
):
    loc, tm = lax.axis_index("loc"), lax.axis_index("tm")
    rows, cols = obs.shape
    n_chip = n_loc // 2
    chip, core = loc // 2, lax.rem(loc, 2)
    sibling = chip * 2 + (1 - core)
    space_length = space_reach / math.sqrt(pos.shape[1])
    time_length = time_reach / stamps.shape[1]
    tm_peers = [lax.rem(tm + d, n_tm) for d in range(1, n_tm)]
    loc_peers = [lax.rem(loc + d, n_loc) for d in range(1, n_loc)]
    mates = [lax.rem(chip + d, n_chip) * 2 + core for d in range(1, n_chip)]
    started = []

    barrier = pltpu.get_barrier_semaphore()
    for peer in tm_peers:
        pl.semaphore_signal(barrier, inc=1, device_id={"tm": peer}, device_id_type=MESH)
    for peer in loc_peers:
        pl.semaphore_signal(barrier, inc=1, device_id={"loc": peer}, device_id_type=MESH)

    def send(ref, slot, send_sem, recv_sems, where):
        copy = pltpu.make_async_remote_copy(
            src_ref=ref.at[slot],
            dst_ref=ref.at[slot],
            send_sem=send_sem,
            recv_sem=recv_sems.at[slot],
            device_id=where,
            device_id_type=MESH,
        )
        copy.start()
        started.append(copy)

    def arrived(ref, slot, recv_sems, send_sem):
        pltpu.make_async_remote_copy(
            src_ref=ref.at[slot],
            dst_ref=ref.at[slot],
            send_sem=send_sem,
            recv_sem=recv_sems.at[slot],
            device_id={"loc": sibling},
            device_id_type=MESH,
        ).wait_recv()

    def lanes(index, width):
        return pl.ds(pl.multiple_of(index * width, width), width)

    mask_float = mask[...].astype(F32)
    first = mask_float * obs[...]
    held[0, tm, pl.ds(0, rows), :] = first
    held[0, tm, pl.ds(rows, SCALARS), :] = jnp.zeros((SCALARS, cols), F32)

    own_stamps = stamps[:, lanes(tm, cols)]

    def time_part(k, carry):
        there = lanes(k, cols)
        distance = jnp.abs(column_of(stamps[:, there], cols) - own_stamps)
        high, low = split(matern_of(distance, time_length))
        kt[0, there, :] = high
        kt[1, there, :] = low
        return carry

    lax.fori_loop(0, n_tm, time_part, 0)

    pl.semaphore_wait(barrier, n_tm - 1 + n_loc - 1)

    def send_held(turn):
        for d, peer in enumerate(tm_peers):
            send(held.at[turn], tm, held_send.at[turn, d], held_recv.at[turn], {"tm": peer})

    def fold(turn):
        def part(slot):
            high, low = split(held[turn, slot, pl.ds(0, rows), :])
            there = lanes(slot, cols)
            return dot3(high, low, kt[0, there, :], kt[1, there, :])

        total = part(tm)
        scalars = held[turn, tm, pl.ds(rows, SCALARS), :]
        for d, peer in enumerate(tm_peers):
            arrived(held.at[turn], peer, held_recv.at[turn], held_send.at[turn, d])
            total += part(peer)
            scalars += held[turn, peer, pl.ds(rows, SCALARS), :]
        inner[turn, loc, pl.ds(0, rows), :] = total
        inner[turn, loc, pl.ds(rows, SCALARS), :] = scalars

    def send_inner(turn):
        send(inner.at[turn], loc, inner_send.at[turn, 0], inner_recv.at[turn], {"loc": sibling})
        for d, peer in enumerate(mates):
            send(inner.at[turn], loc, inner_send.at[turn, d + 1], inner_recv.at[turn], {"loc": peer})

    def mix(turn):
        def part(slot):
            high, low = split(inner[turn, slot, pl.ds(0, rows), :])
            there = lanes(slot, rows)
            return dot3(ks[0, :, there], ks[1, :, there], high, low)

        def scalars_of(slot):
            return inner[turn, slot, pl.ds(rows, SCALARS), :]

        total, scalars = part(loc), scalars_of(loc)
        arrived(inner.at[turn], sibling, inner_recv.at[turn], inner_send.at[turn, 0])
        total, scalars = total + part(sibling), scalars + scalars_of(sibling)
        for d, peer in enumerate(mates):
            arrived(inner.at[turn], peer, inner_recv.at[turn], inner_send.at[turn, 0])
            send(inner.at[turn], peer, pass_send.at[turn, d], inner_recv.at[turn], {"loc": sibling})
            total, scalars = total + part(peer), scalars + scalars_of(peer)
        for d, peer in enumerate(mates):
            slot = (peer - core) + (1 - core)
            arrived(inner.at[turn], slot, inner_recv.at[turn], inner_send.at[turn, 0])
            total, scalars = total + part(slot), scalars + scalars_of(slot)
        return total, scalars

    def predict(turn):
        def part(slot, total):
            high, low = split(inner[turn, slot, pl.ds(0, rows), :])
            there = lanes(slot, rows)
            return total + dot3(kx[0, :, there], kx[1, :, there], high, low)

        return lax.fori_loop(0, n_loc, part, jnp.zeros((rows, cols), F32))

    def space_kernel(out, x_column, y_column):
        def part(k, carry):
            there = lanes(k, rows)
            dx = x_column - pos[0:1, there]
            dy = y_column - pos[1:2, there]
            high, low = split(matern_of(jnp.sqrt(dx * dx + dy * dy), space_length))
            out[0, :, there] = high
            out[1, :, there] = low
            return carry

        lax.fori_loop(0, n_loc, part, 0)

    send_held(0)
    own = lanes(loc, rows)
    space_kernel(ks, column_of(pos[0:1, own], rows), column_of(pos[1:2, own], rows))
    fold(0)
    send_inner(0)

    wanted = column_of(order[:, own].astype(F32), rows)
    lane = lax.broadcasted_iota(jnp.int32, (rows, rows), 1).astype(F32)

    def pick(k, carry):
        x, y = carry
        there = lanes(k, rows)
        hit = wanted == lane + lax.convert_element_type(k * rows, F32)
        x += jnp.where(hit, test[0:1, there], 0.0)
        y += jnp.where(hit, test[1:2, there], 0.0)
        return x, y

    zero = jnp.zeros((rows, rows), F32)
    x_test, y_test = lax.fori_loop(0, test.shape[1] // rows, pick, (zero, zero))
    x_test = jnp.sum(x_test, axis=1, keepdims=True)
    y_test = jnp.sum(y_test, axis=1, keepdims=True)
    space_kernel(kx, x_test, y_test)

    noise_row = noise[...]
    outer, _ = mix(0)
    image = mask_float * outer * amplitude + first * noise_row

    held[1, tm, pl.ds(0, rows), :] = image
    held[1, tm, pl.ds(rows, SCALARS), :] = lane_sums(first * first, first * image, image * image)
    send_held(1)
    predicted_first = predict(0)
    fold(1)
    send_inner(1)
    outer, scalars = mix(1)
    image_image = mask_float * outer * amplitude + image * noise_row

    sums = jnp.sum(scalars, axis=1, keepdims=True)
    norm, curvature, image_norm = sums[0:1], sums[1:2], sums[2:3]
    step = norm / curvature
    ratio = jnp.maximum(step * (step * image_norm) - norm, 0.0) / norm
    residual = first - step * image
    direction = residual + ratio * first
    direction_image = (image - step * image_image) + ratio * image

    red_t[tm] = lane_sums(residual * residual, direction * direction_image)
    for d, peer in enumerate(tm_peers):
        send(red_t, tm, rt_send.at[d], rt_recv, {"tm": peer})
    predicted_image = predict(1)
    for d, peer in enumerate(tm_peers):
        arrived(red_t, peer, rt_recv, rt_send.at[d])
    red_l[loc] = jnp.sum(red_t[...], axis=0)
    for d, peer in enumerate(loc_peers):
        send(red_l, loc, rl_send.at[d], rl_recv, {"loc": peer})
    for d, peer in enumerate(loc_peers):
        arrived(red_l, peer, rl_recv, rl_send.at[d])
    sums = jnp.sum(jnp.sum(red_l[...], axis=0), axis=1, keepdims=True)
    last_step = sums[0:1] / sums[1:2]

    est[...] = step * first + last_step * direction
    on_first = amplitude * (step + last_step * (1.0 + ratio))
    on_image = amplitude * (-last_step * step)
    post[...] = on_first * predicted_first + on_image * predicted_image
    for copy in started:
        copy.wait_send()


def solution(mesh):
    n_loc, n_tm = mesh.shape["loc"], mesh.shape["tm"]

    def on_device(observed, observed_mask, positions, time_stamps, noise_var, test_coords, site_order):
        rows, cols = observed.shape
        locs, times = positions.shape[1], time_stamps.shape[0]
        block = jax.ShapeDtypeStruct((rows, cols), F32)
        vmem = pl.BlockSpec(memory_space=pltpu.VMEM)
        dma = pltpu.SemaphoreType.DMA
        return pl.pallas_call(
            functools.partial(kernel, n_loc, n_tm),
            out_shape=(block, block),
            in_specs=[vmem] * 7,
            out_specs=(vmem, vmem),
            scratch_shapes=[
                pltpu.VMEM((2, n_tm, rows + SCALARS, cols), F32),
                pltpu.VMEM((2, n_loc, rows + SCALARS, cols), F32),
                pltpu.VMEM((n_tm, SCALARS, cols), F32),
                pltpu.VMEM((n_loc, SCALARS, cols), F32),
                pltpu.VMEM((2, rows, locs), BF16),
                pltpu.VMEM((2, rows, locs), BF16),
                pltpu.VMEM((2, times, cols), BF16),
                dma((2, n_tm)), dma((2, n_tm)),
                dma((2, n_loc)), dma((2, n_loc)), dma((2, n_loc)),
                dma((n_tm,)), dma((n_tm,)),
                dma((n_loc,)), dma((n_loc,)),
            ],
            compiler_params=pltpu.CompilerParams(
                collective_id=0, has_side_effects=True, vmem_limit_bytes=32 * 1024 * 1024
            ),
        )(
            observed, observed_mask, positions, time_stamps[None, :], noise_var[None, :],
            test_coords, site_order[None, :],
        )

    in_specs = (P("loc", "tm"), P("loc", "tm"), P(), P(), P("tm"), P(), P())
    out_specs = (P("loc", "tm"), P("loc", "tm"))
    return jax.shard_map(on_device, mesh=mesh, in_specs=in_specs, out_specs=out_specs, check_vma=False)
```

```python
import functools
import math

import jax
import jax.numpy as jnp
from jax import lax
from jax.experimental import pallas as pl
from jax.experimental.pallas import tpu as pltpu
from jax.sharding import PartitionSpec as P

MESH = pl.DeviceIdType.MESH
F32 = jnp.float32
BF16 = jnp.bfloat16

root_three = math.sqrt(3.0)
space_reach = 2.5
time_reach = 5.0
amplitude = 0.1
SCALARS = 8
CHUNKS = 2


def split(x):
    high = x.astype(BF16)
    return high, (x - high.astype(F32)).astype(BF16)


def dot(a, b):
    return jnp.dot(a, b, preferred_element_type=F32)


def dot3(a_high, a_low, b_high, b_low):
    return dot(a_high, b_high) + (dot(a_high, b_low) + dot(a_low, b_high))


def column_of(row, width):
    return jnp.transpose(jnp.broadcast_to(row, (width, row.shape[1])))


def matern_of(distance, length):
    scaled = distance * (root_three / length)
    return (1.0 + scaled) * jnp.exp(-scaled)


def lane_sums(*arrays):
    sums = [jnp.sum(a, axis=0, keepdims=True) for a in arrays]
    sums.append(jnp.zeros((SCALARS - len(sums), sums[0].shape[1]), F32))
    return jnp.concatenate(sums, axis=0)


def other(index, step, count):
    if count & (count - 1):
        return lax.rem(index + step, count)
    bit = 1
    while bit < count:
        if step & bit:
            index = index + bit * (1 - 2 * lax.rem(index // bit, 2))
        bit *= 2
    return index


def kernel(
    n_loc, n_tm,
    obs_hbm, mask_hbm, pos_hbm, stamps_hbm, noise_hbm, test_hbm, order_hbm,
    est, post,
    obs, mask, pos, stamps, noise, test, order, arg_sem,
    held, inner, red, kk, kt,
    held_send, held_recv, inner_send, inner_recv, pass_send, red_send, red_recv,
):
    loc, tm = lax.axis_index("loc"), lax.axis_index("tm")
    rows, cols = obs.shape
    n_chip = n_loc // 2
    chip, core = loc // 2, lax.rem(loc, 2)
    sibling = chip * 2 + (1 - core)
    space_length = space_reach / math.sqrt(pos.shape[1])
    time_length = time_reach / stamps.shape[1]
    tm_peers = [other(tm, d, n_tm) for d in range(n_tm - 1, 0, -1)]
    loc_peers = [other(loc, d, n_loc) for d in range(n_loc - 1, 0, -1)]
    mates = [other(chip, d, n_chip) * 2 + core for d in range(n_chip - 1, 0, -1)]
    chunk = rows // CHUNKS
    chunks = [
        pl.ds(h * chunk, chunk + (SCALARS if h == CHUNKS - 1 else 0)) for h in range(CHUNKS)
    ]
    started = []

    arguments = (
        (stamps_hbm, stamps), (obs_hbm, obs), (mask_hbm, mask), (pos_hbm, pos),
        (test_hbm, test), (order_hbm, order), (noise_hbm, noise),
    )
    loads = [
        pltpu.make_async_copy(there, here, arg_sem.at[k]) for k, (there, here) in enumerate(arguments)
    ]
    for load in loads:
        load.start()

    barrier = pltpu.get_barrier_semaphore()
    for peer in tm_peers:
        pl.semaphore_signal(barrier, inc=1, device_id={"tm": peer}, device_id_type=MESH)
    for peer in loc_peers:
        pl.semaphore_signal(barrier, inc=1, device_id={"loc": peer}, device_id_type=MESH)

    def copy_of(ref, slot, h, send_sem, recv_sem, where):
        block = ref.at[slot, chunks[h], :]
        return pltpu.make_async_remote_copy(
            src_ref=block,
            dst_ref=block,
            send_sem=send_sem,
            recv_sem=recv_sem.at[slot, h],
            device_id=where,
            device_id_type=MESH,
        )

    def send(*how):
        copy = copy_of(*how)
        copy.start()
        started.append(copy)

    def lanes(index, width):
        return pl.ds(pl.multiple_of(index * width, width), width)

    loads[0].wait()
    loads[1].wait()
    loads[2].wait()
    mask_float = mask[...].astype(F32)
    first = mask_float * obs[...]
    held[0, tm, pl.ds(0, rows), :] = first
    held[0, tm, pl.ds(rows, SCALARS), :] = jnp.zeros((SCALARS, cols), F32)

    own_stamps = stamps[:, lanes(tm, cols)]

    def time_part(k, carry):
        there = lanes(k, cols)
        distance = jnp.abs(column_of(stamps[:, there], cols) - own_stamps)
        high, low = split(matern_of(distance, time_length))
        kt[0, there, :] = high
        kt[1, there, :] = low
        return carry

    lax.fori_loop(0, n_tm, time_part, 0)

    pl.semaphore_wait(barrier, n_tm - 1 + n_loc - 1)

    def send_held(turn):
        for h in range(CHUNKS):
            for d, peer in enumerate(tm_peers):
                send(held.at[turn], tm, h, held_send.at[turn, d, h], held_recv.at[turn], {"tm": peer})

    def fold(turn):
        scalars = held[turn, tm, pl.ds(rows, SCALARS), :]
        for h in range(CHUNKS):
            these = pl.ds(h * chunk, chunk)

            def part(slot):
                high, low = split(held[turn, slot, these, :])
                there = lanes(slot, cols)
                return dot3(high, low, kt[0, there, :], kt[1, there, :])

            total = part(tm)
            for d, peer in reversed(list(enumerate(tm_peers))):
                copy_of(
                    held.at[turn], peer, h, held_send.at[turn, d, h], held_recv.at[turn], {"tm": peer}
                ).wait_recv()
                total += part(peer)
                if h == CHUNKS - 1:
                    scalars += held[turn, peer, pl.ds(rows, SCALARS), :]
            inner[turn, loc, these, :] = total
            if h == CHUNKS - 1:
                inner[turn, loc, pl.ds(rows, SCALARS), :] = scalars
            for d, peer in enumerate(mates + [sibling]):
                send(inner.at[turn], loc, h, inner_send.at[turn, d, h], inner_recv.at[turn], {"loc": peer})

    def mix(turn):
        def part(slot):
            high, low = split(inner[turn, slot, pl.ds(0, rows), :])
            there = lanes(slot, rows)
            return dot3(kk[0, :, there], kk[1, :, there], high, low)

        def scalars_of(slot):
            return inner[turn, slot, pl.ds(rows, SCALARS), :]

        def arrived(slot, h):
            copy_of(
                inner.at[turn], slot, h, inner_send.at[turn, 0, 0], inner_recv.at[turn], {"loc": sibling}
            ).wait_recv()

        total, scalars = part(loc), scalars_of(loc)
        for h in range(CHUNKS):
            arrived(sibling, h)
        total, scalars = total + part(sibling), scalars + scalars_of(sibling)
        for h in range(CHUNKS):
            for d, peer in enumerate(mates):
                arrived(peer, h)
                send(inner.at[turn], peer, h, pass_send.at[turn, d, h], inner_recv.at[turn], {"loc": sibling})
        for peer in mates:
            total, scalars = total + part(peer), scalars + scalars_of(peer)
        for peer in mates:
            slot = (peer - core) + (1 - core)
            for h in range(CHUNKS):
                arrived(slot, h)
            total, scalars = total + part(slot), scalars + scalars_of(slot)
        return total[:rows], total[rows:], scalars

    def space_kernel(these, x_column, y_column):
        def part(k, carry):
            there = lanes(k, rows)
            dx = x_column - pos[0:1, there]
            dy = y_column - pos[1:2, there]
            high, low = split(matern_of(jnp.sqrt(dx * dx + dy * dy), space_length))
            kk[0, these, there] = high
            kk[1, these, there] = low
            return carry

        lax.fori_loop(0, n_loc, part, 0)

    send_held(0)
    for load in loads[3:]:
        load.wait()
    own = lanes(loc, rows)
    space_kernel(pl.ds(0, rows), column_of(pos[0:1, own], rows), column_of(pos[1:2, own], rows))
    fold(0)

    wanted = column_of(order[:, own].astype(F32), rows)
    lane = lax.broadcasted_iota(jnp.int32, (rows, rows), 1).astype(F32)

    def pick(k, carry):
        x, y = carry
        there = lanes(k, rows)
        hit = wanted == lane + lax.convert_element_type(k * rows, F32)
        x += jnp.where(hit, test[0:1, there], 0.0)
        y += jnp.where(hit, test[1:2, there], 0.0)
        return x, y

    zero = jnp.zeros((rows, rows), F32)
    x_test, y_test = lax.fori_loop(0, test.shape[1] // rows, pick, (zero, zero))
    x_test = jnp.sum(x_test, axis=1, keepdims=True)
    y_test = jnp.sum(y_test, axis=1, keepdims=True)
    space_kernel(pl.ds(rows, rows), x_test, y_test)

    noise_row = noise[...]
    outer, predicted_first, _ = mix(0)
    image = mask_float * outer * amplitude + first * noise_row

    held[1, tm, pl.ds(0, rows), :] = image
    held[1, tm, pl.ds(rows, SCALARS), :] = lane_sums(first * first, first * image, image * image)
    send_held(1)
    fold(1)
    outer, predicted_image, scalars = mix(1)
    image_image = mask_float * outer * amplitude + image * noise_row

    sums = jnp.sum(scalars, axis=1, keepdims=True)
    norm, curvature, image_norm = sums[0:1], sums[1:2], sums[2:3]
    step = norm / curvature
    ratio = jnp.maximum(step * (step * image_norm) - norm, 0.0) / norm
    residual = first - step * image
    direction = residual + ratio * first
    direction_image = (image - step * image_image) + ratio * image

    red[0] = lane_sums(residual * residual, direction * direction_image)
    far = [(a, b) for b in range(n_tm - 1, -1, -1) for a in range(n_loc - 1, -1, -1) if a or b]
    for k, (a, b) in enumerate(far):
        copy = pltpu.make_async_remote_copy(
            src_ref=red.at[0],
            dst_ref=red.at[k + 1],
            send_sem=red_send.at[k],
            recv_sem=red_recv,
            device_id=(other(loc, a, n_loc) if a else loc, other(tm, b, n_tm) if b else tm),
            device_id_type=MESH,
        )
        copy.start()
        started.append(copy)
    others = red.at[pl.ds(1, len(far))]
    pltpu.make_async_remote_copy(
        src_ref=others,
        dst_ref=others,
        send_sem=red_send.at[0],
        recv_sem=red_recv,
        device_id={"loc": sibling},
        device_id_type=MESH,
    ).wait_recv()
    sums = jnp.sum(jnp.sum(red[...], axis=0), axis=1, keepdims=True)
    last_step = sums[0:1] / sums[1:2]

    est[...] = step * first + last_step * direction
    on_first = amplitude * (step + last_step * (1.0 + ratio))
    on_image = amplitude * (-last_step * step)
    post[...] = on_first * predicted_first + on_image * predicted_image
    for copy in started:
        copy.wait_send()


def solution(mesh):
    n_loc, n_tm = mesh.shape["loc"], mesh.shape["tm"]

    def on_device(observed, observed_mask, positions, time_stamps, noise_var, test_coords, site_order):
        rows, cols = observed.shape
        locs, times = positions.shape[1], time_stamps.shape[0]
        block = jax.ShapeDtypeStruct((rows, cols), F32)
        vmem = pl.BlockSpec(memory_space=pltpu.VMEM)
        dma = pltpu.SemaphoreType.DMA
        return pl.pallas_call(
            functools.partial(kernel, n_loc, n_tm),
            out_shape=(block, block),
            in_specs=[pl.BlockSpec(memory_space=pltpu.HBM)] * 7,
            out_specs=(vmem, vmem),
            scratch_shapes=[
                pltpu.VMEM((rows, cols), F32),
                pltpu.VMEM((rows, cols), jnp.int32),
                pltpu.VMEM((2, locs), F32),
                pltpu.VMEM((1, times), F32),
                pltpu.VMEM((1, cols), F32),
                pltpu.VMEM(test_coords.shape, F32),
                pltpu.VMEM((1, site_order.shape[0]), jnp.int32),
                dma((7,)),
                pltpu.VMEM((2, n_tm, rows + SCALARS, cols), F32),
                pltpu.VMEM((2, n_loc, rows + SCALARS, cols), F32),
                pltpu.VMEM((n_loc * n_tm, SCALARS, cols), F32),
                pltpu.VMEM((2, 2 * rows, locs), BF16),
                pltpu.VMEM((2, times, cols), BF16),
                dma((2, n_tm, CHUNKS)), dma((2, n_tm, CHUNKS)),
                dma((2, n_loc, CHUNKS)), dma((2, n_loc, CHUNKS)), dma((2, n_loc, CHUNKS)),
                dma((n_loc * n_tm,)), dma(()),
            ],
            compiler_params=pltpu.CompilerParams(
                collective_id=0, has_side_effects=True, vmem_limit_bytes=60 * 1024 * 1024
            ),
        )(
            observed, observed_mask, positions, time_stamps[None, :], noise_var[None, :],
            test_coords, site_order[None, :],
        )

    in_specs = (P("loc", "tm"), P("loc", "tm"), P(), P(), P("tm"), P(), P())
    out_specs = (P("loc", "tm"), P("loc", "tm"))
    return jax.shard_map(on_device, mesh=mesh, in_specs=in_specs, out_specs=out_specs, check_vma=False)
```

```python
import functools
import math

import jax
import jax.numpy as jnp
from jax import lax
from jax.experimental import pallas as pl
from jax.experimental.pallas import tpu as pltpu
from jax.sharding import PartitionSpec as P

MESH = pl.DeviceIdType.MESH
F32 = jnp.float32
BF16 = jnp.bfloat16

root_three = math.sqrt(3.0)
space_reach = 2.5
time_reach = 5.0
amplitude = 0.1
SCALARS = 8
SIXTEENTHS = (0, 8, 16)
CHUNKS = len(SIXTEENTHS) - 1


def split(x):
    high = x.astype(BF16)
    return high, (x - high.astype(F32)).astype(BF16)


def dot(a, b):
    return jnp.dot(a, b, preferred_element_type=F32)


def dot3(a_high, a_low, b_high, b_low):
    return dot(a_high, b_high) + (dot(a_high, b_low) + dot(a_low, b_high))


def column_of(row, width):
    return jnp.transpose(jnp.broadcast_to(row, (width, row.shape[1])))


def matern_of(distance, length):
    scaled = distance * (root_three / length)
    return (1.0 + scaled) * jnp.exp(-scaled)


def lane_sums(*arrays):
    sums = [jnp.sum(a, axis=0, keepdims=True) for a in arrays]
    sums.append(jnp.zeros((SCALARS - len(sums), sums[0].shape[1]), F32))
    return jnp.concatenate(sums, axis=0)


def other(index, step, count):
    if count & (count - 1):
        return lax.rem(index + step + count, count)
    step = abs(step)
    bit = 1
    while bit < count:
        if step & bit:
            index = index + bit * (1 - 2 * lax.rem(index // bit, 2))
        bit *= 2
    return index


def kernel(
    n_loc, n_tm,
    obs_hbm, mask_hbm, pos_hbm, stamps_hbm, noise_hbm, test_hbm, order_hbm,
    est, post,
    obs, mask, pos, stamps, noise, test, order, arg_sem,
    held, inner, red, kk, kt,
    held_send, held_recv, inner_send, inner_recv, pass_send, red_send, red_recv,
):
    loc, tm = lax.axis_index("loc"), lax.axis_index("tm")
    rows, cols = obs.shape
    n_chip = n_loc // 2
    chip, core = loc // 2, lax.rem(loc, 2)
    sibling = chip * 2 + (1 - core)
    space_length = space_reach / math.sqrt(pos.shape[1])
    time_length = time_reach / stamps.shape[1]
    tm_peers = [other(tm, d, n_tm) for d in range(n_tm - 1, 0, -1)]
    loc_peers = [other(loc, d, n_loc) for d in range(n_loc - 1, 0, -1)]
    near = []
    far = list(range(n_chip - 1, 0, -1))
    starts = [rows * part // 16 for part in SIXTEENTHS]
    parts = [pl.ds(starts[h], starts[h + 1] - starts[h]) for h in range(CHUNKS)]
    chunks = parts[:-1] + [pl.ds(starts[-2], rows + SCALARS - starts[-2])]
    started = []

    barrier = pltpu.get_barrier_semaphore()
    for peer in tm_peers:
        pl.semaphore_signal(barrier, inc=1, device_id={"tm": peer}, device_id_type=MESH)
    for peer in loc_peers:
        pl.semaphore_signal(barrier, inc=1, device_id={"loc": peer}, device_id_type=MESH)

    arguments = (
        (stamps_hbm, stamps), (obs_hbm, obs), (mask_hbm, mask), (pos_hbm, pos),
        (test_hbm, test), (order_hbm, order), (noise_hbm, noise),
    )
    loads = [
        pltpu.make_async_copy(there, here, arg_sem.at[k]) for k, (there, here) in enumerate(arguments)
    ]
    for load in loads:
        load.start()

    def copy_of(ref, slot, h, send_sem, recv_sem, where):
        block = ref.at[slot, chunks[h], :]
        return pltpu.make_async_remote_copy(
            src_ref=block,
            dst_ref=block,
            send_sem=send_sem,
            recv_sem=recv_sem.at[slot, h],
            device_id=where,
            device_id_type=MESH,
        )

    def send(*how):
        copy = copy_of(*how)
        copy.start()
        started.append(copy)

    def lanes(index, width):
        return pl.ds(pl.multiple_of(index * width, width), width)

    loads[0].wait()
    loads[1].wait()
    loads[2].wait()
    mask_float = mask[...].astype(F32)
    first = mask_float * obs[...]
    held[0, tm, pl.ds(0, rows), :] = first
    held[0, tm, pl.ds(rows, SCALARS), :] = jnp.zeros((SCALARS, cols), F32)

    own_stamps = stamps[:, lanes(tm, cols)]

    def time_part(k, carry):
        there = lanes(k, cols)
        distance = jnp.abs(column_of(stamps[:, there], cols) - own_stamps)
        high, low = split(matern_of(distance, time_length))
        kt[0, there, :] = high
        kt[1, there, :] = low
        return carry

    lax.fori_loop(0, n_tm, time_part, 0)

    pl.semaphore_wait(barrier, n_tm - 1 + n_loc - 1)

    def send_held(turn):
        for h in range(CHUNKS):
            for d, peer in enumerate(tm_peers):
                send(held.at[turn], tm, h, held_send.at[turn, d, h], held_recv.at[turn], {"tm": peer})

    def fold(turn):
        scalars = held[turn, tm, pl.ds(rows, SCALARS), :]
        for h in range(CHUNKS):
            these = parts[h]

            def part(slot):
                high, low = split(held[turn, slot, these, :])
                there = lanes(slot, cols)
                return dot3(high, low, kt[0, there, :], kt[1, there, :])

            total = part(tm)
            for d, peer in reversed(list(enumerate(tm_peers))):
                copy_of(
                    held.at[turn], peer, h, held_send.at[turn, d, h], held_recv.at[turn], {"tm": peer}
                ).wait_recv()
                total += part(peer)
                if h == CHUNKS - 1:
                    scalars += held[turn, peer, pl.ds(rows, SCALARS), :]
            inner[turn, loc, these, :] = total
            if h == CHUNKS - 1:
                inner[turn, loc, pl.ds(rows, SCALARS), :] = scalars
            targets = [other(chip, d, n_chip) * 2 + core for d in far]
            for d in near:
                there = other(chip, d, n_chip) * 2
                targets += [there + core, there + (1 - core)]
            for d, peer in enumerate(targets + [sibling]):
                send(inner.at[turn], loc, h, inner_send.at[turn, d, h], inner_recv.at[turn], {"loc": peer})

    def mix(turn):
        def part(slot):
            high, low = split(inner[turn, slot, pl.ds(0, rows), :])
            there = lanes(slot, rows)
            return dot3(kk[0, :, there], kk[1, :, there], high, low)

        def scalars_of(slot):
            return inner[turn, slot, pl.ds(rows, SCALARS), :]

        def arrived(slot, h):
            copy_of(
                inner.at[turn], slot, h, inner_send.at[turn, 0, 0], inner_recv.at[turn], {"loc": sibling}
            ).wait_recv()

        passed = [other(chip, -d, n_chip) * 2 for d in far]
        direct = [other(chip, -d, n_chip) * 2 for d in near]
        for h in range(CHUNKS):
            for d, pair in enumerate(passed):
                arrived(pair + core, h)
                send(
                    inner.at[turn], pair + core, h, pass_send.at[turn, d, h], inner_recv.at[turn],
                    {"loc": sibling},
                )
        total, scalars = part(loc), scalars_of(loc)
        for h in range(CHUNKS):
            arrived(sibling, h)
        for slot in [sibling] + [pair + core for pair in passed]:
            total, scalars = total + part(slot), scalars + scalars_of(slot)
        last = [pair + k for pair in direct for k in (0, 1)] + [pair + (1 - core) for pair in passed]
        for slot in last:
            for h in range(CHUNKS):
                arrived(slot, h)
            total, scalars = total + part(slot), scalars + scalars_of(slot)
        return total[:rows], total[rows:], scalars

    def space_kernel(these, x_column, y_column):
        def part(k, carry):
            there = lanes(k, rows)
            dx = x_column - pos[0:1, there]
            dy = y_column - pos[1:2, there]
            high, low = split(matern_of(jnp.sqrt(dx * dx + dy * dy), space_length))
            kk[0, these, there] = high
            kk[1, these, there] = low
            return carry

        lax.fori_loop(0, n_loc, part, 0)

    send_held(0)
    for load in loads[3:]:
        load.wait()
    own = lanes(loc, rows)
    space_kernel(pl.ds(0, rows), column_of(pos[0:1, own], rows), column_of(pos[1:2, own], rows))
    fold(0)

    wanted = column_of(order[:, own].astype(F32), rows)
    lane = lax.broadcasted_iota(jnp.int32, (rows, rows), 1).astype(F32)

    def pick(k, carry):
        x, y = carry
        there = lanes(k, rows)
        hit = wanted == lane + lax.convert_element_type(k * rows, F32)
        x += jnp.where(hit, test[0:1, there], 0.0)
        y += jnp.where(hit, test[1:2, there], 0.0)
        return x, y

    zero = jnp.zeros((rows, rows), F32)
    x_test, y_test = lax.fori_loop(0, test.shape[1] // rows, pick, (zero, zero))
    x_test = jnp.sum(x_test, axis=1, keepdims=True)
    y_test = jnp.sum(y_test, axis=1, keepdims=True)
    space_kernel(pl.ds(rows, rows), x_test, y_test)

    noise_row = noise[...]
    outer, predicted_first, _ = mix(0)
    image = mask_float * outer * amplitude + first * noise_row

    held[1, tm, pl.ds(0, rows), :] = image
    held[1, tm, pl.ds(rows, SCALARS), :] = lane_sums(first * first, first * image, image * image)
    send_held(1)
    fold(1)
    outer, predicted_image, scalars = mix(1)
    image_image = mask_float * outer * amplitude + image * noise_row

    sums = jnp.sum(scalars, axis=1, keepdims=True)
    norm, curvature, image_norm = sums[0:1], sums[1:2], sums[2:3]
    step = norm / curvature
    ratio = jnp.maximum(step * (step * image_norm) - norm, 0.0) / norm
    residual = first - step * image
    direction = residual + ratio * first
    direction_image = (image - step * image_image) + ratio * image

    red[0] = lane_sums(residual * residual, direction * direction_image)
    away = [(a, b) for b in range(n_tm - 1, -1, -1) for a in range(n_loc - 1, -1, -1) if a or b]
    for k, (a, b) in enumerate(away):
        copy = pltpu.make_async_remote_copy(
            src_ref=red.at[0],
            dst_ref=red.at[k + 1],
            send_sem=red_send.at[k],
            recv_sem=red_recv,
            device_id=(other(loc, a, n_loc) if a else loc, other(tm, b, n_tm) if b else tm),
            device_id_type=MESH,
        )
        copy.start()
        started.append(copy)
    others = red.at[pl.ds(1, len(away))]
    pltpu.make_async_remote_copy(
        src_ref=others,
        dst_ref=others,
        send_sem=red_send.at[0],
        recv_sem=red_recv,
        device_id={"loc": sibling},
        device_id_type=MESH,
    ).wait_recv()
    sums = jnp.sum(jnp.sum(red[...], axis=0), axis=1, keepdims=True)
    last_step = sums[0:1] / sums[1:2]

    est[...] = step * first + last_step * direction
    on_first = amplitude * (step + last_step * (1.0 + ratio))
    on_image = amplitude * (-last_step * step)
    post[...] = on_first * predicted_first + on_image * predicted_image
    for copy in started:
        copy.wait_send()


def solution(mesh):
    n_loc, n_tm = mesh.shape["loc"], mesh.shape["tm"]

    def on_device(observed, observed_mask, positions, time_stamps, noise_var, test_coords, site_order):
        rows, cols = observed.shape
        locs, times = positions.shape[1], time_stamps.shape[0]
        vmem = pl.BlockSpec(memory_space=pltpu.VMEM)
        dma = pltpu.SemaphoreType.DMA
        return pl.pallas_call(
            functools.partial(kernel, n_loc, n_tm),
            out_shape=(pltpu.VMEM((rows, cols), F32), pltpu.VMEM((rows, cols), F32)),
            in_specs=[pl.BlockSpec(memory_space=pltpu.HBM)] * 7,
            out_specs=(vmem, vmem),
            scratch_shapes=[
                pltpu.VMEM((rows, cols), F32),
                pltpu.VMEM((rows, cols), jnp.int32),
                pltpu.VMEM((2, locs), F32),
                pltpu.VMEM((1, times), F32),
                pltpu.VMEM((1, cols), F32),
                pltpu.VMEM(test_coords.shape, F32),
                pltpu.VMEM((1, site_order.shape[0]), jnp.int32),
                dma((7,)),
                pltpu.VMEM((2, n_tm, rows + SCALARS, cols), F32),
                pltpu.VMEM((2, n_loc, rows + SCALARS, cols), F32),
                pltpu.VMEM((n_loc * n_tm, SCALARS, cols), F32),
                pltpu.VMEM((2, 2 * rows, locs), BF16),
                pltpu.VMEM((2, times, cols), BF16),
                dma((2, n_tm, CHUNKS)), dma((2, n_tm, CHUNKS)),
                dma((2, n_loc, CHUNKS)), dma((2, n_loc, CHUNKS)), dma((2, n_loc, CHUNKS)),
                dma((n_loc * n_tm,)), dma(()),
            ],
            compiler_params=pltpu.CompilerParams(
                collective_id=0, has_side_effects=True, vmem_limit_bytes=60 * 1024 * 1024
            ),
        )(
            observed, observed_mask, positions, time_stamps[None, :], noise_var[None, :],
            test_coords, site_order[None, :],
        )

    in_specs = (P("loc", "tm"), P("loc", "tm"), P(), P(), P("tm"), P(), P())
    out_specs = (P("loc", "tm"), P("loc", "tm"))
    return jax.shard_map(on_device, mesh=mesh, in_specs=in_specs, out_specs=out_specs, check_vma=False)
```
